128 devices in a mesh: aux: 8 (over z, core), bas: 16 (over y, x).
Axes of the slice: x: 4, y: 4, z: 4, core: 2. Of those that a mesh axis runs over, the one named last changes fastest.
Arguments:
- three_index: bfloat16 [6144, 32, 4096], P(('aux', 'bas')), may hold values from -6 to 6
- block_size: int32 [32], replicated, may hold values from 64 to 128, as said below
- screen: int32 [32, 5], replicated, may hold values from 0 to 1, as said below
Outputs:
- exchange_band: float32 [4096, 1152], P(('bas', 'aux'))
The draws below stay inside these ranges and needn't reach their ends.
Inputs may be any that keep to these rules, and one draw needn't show every extreme that they name: `block_size`: block sizes lie between 64 and 128; some block is full. screen[a, 0] = 1 for every block a; screen[a, d] = 0 wherever a + d >= 32.
All inputs are finite; a program needn't handle non-finite values.
Results may differ from the reference program's by a relative error of at most 0.0038.
Values may be sent and summed in bfloat16 or wider, within the bound.
No kernel may reach another device: no remote copies, remote signals or barrier semaphores. Data moves between devices by JAX's collectives and lax.ppermute only.
A program may use at most 448 MiB of HBM per device.

```python
import math
import jax
import jax.numpy as jnp
from jax import lax

AUX = 6144
OCC = 32
BW = 128
BAND = 5
NB = 32
NBAS = 4096


def draw_block_size(key, part):
    key = jax.random.fold_in(key, 11)
    size_key, pick_key = jax.random.split(key)
    drawn_sizes = jax.random.randint(size_key, (NB,), BW // 2, BW + 1)
    chosen = jax.random.randint(pick_key, (), 0, NB)
    return jnp.where(jnp.arange(NB) == chosen, BW, drawn_sizes).astype(jnp.int32)


def draw_screen(key, part):
    key = jax.random.fold_in(key, 23)
    level_key, pair_key = jax.random.split(key)
    levels = jax.random.randint(level_key, (NB,), 1, 9)
    row_level = levels[jnp.arange(NB) // 2]
    pair_draws = jax.random.randint(pair_key, (NB, BAND), 0, 8)
    kept_pairs = (pair_draws < row_level[:, None]).astype(jnp.int32)
    offset_grid = jnp.arange(BAND)[None, :]
    row_grid = jnp.arange(NB)[:, None]
    kept_pairs = jnp.where(offset_grid == 0, 1, kept_pairs)
    kept_pairs = jnp.where(row_grid + offset_grid >= NB, 0, kept_pairs)
    return kept_pairs.astype(jnp.int32)


def shard_levels(key, shape, shards, low, largest):
    loudness = 1.0
    for dim, blocks in shards:
        draws = jax.random.uniform(jax.random.fold_in(jax.random.fold_in(key, 6), dim), (blocks,), jnp.float32, low / len(shards), largest / len(shards))
        loudness = loudness * jnp.repeat(jnp.exp(draws), shape[dim] // blocks).reshape((-1,) + (1,) * (len(shape) - 1 - dim))
    return loudness


def centred(stream_key, dims, spread, bound, pieces=(), kind=jnp.bfloat16):
    entries = jax.random.normal(stream_key, dims, jnp.float32) * spread
    if len(pieces) > 0:
        entries = shard_levels(stream_key, dims, pieces, -0.22, 0.18) * entries
    return jnp.clip(entries, min=-bound, max=bound).astype(kind)


def setup_inputs(seed: int = 0) -> dict:
    arg_keys = jax.random.split(jax.random.key(seed), 4)
    return {
        "three_index": centred(arg_keys[0], (AUX, OCC, NBAS), 1.0, 6.0, ((0, 128),)),
        "block_size": draw_block_size(jax.random.fold_in(arg_keys[3], 71), 0),
        "screen": draw_screen(jax.random.fold_in(arg_keys[3], 71), 0),
    }


def reference(three_index, block_size, screen):
    total_blocks = screen.shape[0]
    band_width = screen.shape[1]
    flattened = three_index.reshape(AUX * OCC, total_blocks * BW)
    factor = 1.0 / math.sqrt(AUX * OCC)
    position = jnp.arange(BW, dtype=jnp.int32)

    def upper(pair_index):
        row_block = (pair_index // band_width).astype(jnp.int32)
        offset = (pair_index % band_width).astype(jnp.int32)
        partner = jnp.minimum(row_block + offset, total_blocks - 1).astype(jnp.int32)
        left_block = lax.dynamic_slice_in_dim(flattened, row_block * BW, BW, 1)
        right_block = lax.dynamic_slice_in_dim(flattened, partner * BW, BW, 1)
        product = jnp.dot(left_block.T, right_block, preferred_element_type=jnp.float32)
        row_mask = (position < block_size[row_block]).astype(jnp.float32)
        col_mask = (position < block_size[partner]).astype(jnp.float32)
        kept_flag = screen[row_block, offset].astype(jnp.float32)
        return product * (factor * kept_flag) * row_mask[:, None] * col_mask[None, :]
    pair_tiles = lax.map(upper, jnp.arange(total_blocks * band_width, dtype=jnp.int32))
    pair_tiles = pair_tiles.reshape(total_blocks, band_width, BW, BW)
    upper_part = pair_tiles.transpose(0, 2, 1, 3)
    lower_list = []
    for slot in range(band_width - 1):
        offset = band_width - 1 - slot
        moved = jnp.concatenate([jnp.zeros((offset, BW, BW), pair_tiles.dtype), pair_tiles[:total_blocks - offset, offset]], axis=0)
        lower_list.append(moved.transpose(0, 2, 1))
    lower_part = jnp.stack(lower_list, axis=2)
    band_rows = jnp.concatenate([lower_part, upper_part], axis=2)
    return band_rows.reshape(total_blocks * BW, (2 * band_width - 1) * BW)
```

```python
import functools
import math

import jax
import jax.numpy as jnp
from jax import lax
from jax.experimental import pallas as pl
from jax.experimental.pallas import tpu as pltpu
from jax.sharding import PartitionSpec as P

AUX = 6144
OCC = 32
BW = 128
BAND = 5
NB = 32
OWNERS = 16
PAIR = 2 * BW
AXES = ("aux", "bas")
F32 = jnp.float32
BF16 = jnp.bfloat16

TILES = (
    ((0, 0), (0, 2), (0, 3), (1, 1), (1, 2)),
    ((1, 0), (0, 1), (0, 4), (1, 3), (1, 4)),
)
PANEL = {
    (0, 0): ((0, 1, 2, 5, 7), (4, 6, 7, 2, 3)),
    (1, 0): ((1, 2, 6, 7), (5, 8, 0, 1)),
    (0, 1): ((3, 4, 6, 8), (5, 6, 1, 2)),
    (1, 1): ((0, 3, 4, 5, 8), (4, 7, 8, 3, 0)),
}
GROUPS = (
    ((1, 0), (1, 1), (1, 2), (1, 3), (0, 1), (2, 1), (3, 1)),
    ((3, 0), (3, 2), (3, 3), (0, 3), (2, 3)),
    ((2, 0), (2, 2), (0, 2)),
    ((0, 0),),
)


def device(z, c, y, x):
    return (z * 2 + c) * 16 + y * 4 + x


EVERY = [(z, c, y, x) for z in range(4) for c in range(2) for y in range(4) for x in range(4)]


def core_pairs():
    return [(device(z, c, y, x), device(z, 1 - c, y, x)) for z, c, y, x in EVERY]


def plane_pairs(step, first):
    pairs = []
    for z, c, y, x in EVERY:
        if (c == 0) == first:
            target = device(z, c, (y + step) % 4, x)
        else:
            target = device(z, c, y, (x + step) % 4)
        pairs.append((device(z, c, y, x), target))
    return pairs


def mirror_pairs():
    pairs = []
    for z, c, y, x in EVERY:
        owner = y * 4 + x + 1 + c
        if owner < OWNERS:
            pairs.append((device(z, c, y, x), device(z, c, owner // 4, owner % 4)))
    return pairs


def z_pairs(step):
    return [(device(z, c, y, x), device((z + step) % 4, c, y, x)) for z, c, y, x in EVERY]


def send(value, pairs):
    return lax.ppermute(value, AXES, pairs)


def tiles_kernel(owner_ref, place_ref, core_ref, left_ref, next_ref, beyond_ref, mine_ref, theirs_ref):
    left = left_ref[...]
    products = [
        lax.dot_general(left, right, (((0,), (0,)), ((), ())), preferred_element_type=F32)
        for right in (left, next_ref[...], beyond_ref[...])
    ]

    def tile(row, offset):
        slot = row + offset
        part = products[slot // 2]
        return part[row * BW : (row + 1) * BW, (slot % 2) * BW : (slot % 2 + 1) * BW].astype(BF16)

    def put(mine, theirs):
        for place in range(BAND):
            mine_ref[0, place] = tile(*TILES[mine][place])
            theirs_ref[0, place] = tile(*TILES[theirs][place])

    core = core_ref[0]

    @pl.when(core == 0)
    def _():
        put(0, 1)

    @pl.when(core != 0)
    def _():
        put(1, 0)


def partial_tiles(flat, owners, places, core):
    count = len(places)
    depth = flat.shape[0]

    def column(ahead):
        return pl.BlockSpec(
            (depth, PAIR), lambda i, owner, place, core: (0, jnp.minimum(owner[i] + ahead, OWNERS - 1))
        )

    shape = jax.ShapeDtypeStruct((count, BAND, BW, BW), BF16)
    return pl.pallas_call(
        tiles_kernel,
        grid_spec=pltpu.PrefetchScalarGridSpec(
            num_scalar_prefetch=3,
            grid=(count,),
            in_specs=[column(0), column(1), column(2)],
            out_specs=[
                pl.BlockSpec((1, BAND, BW, BW), lambda i, owner, place, core: (i, 0, 0, 0)),
                pl.BlockSpec((1, BAND, BW, BW), lambda i, owner, place, core: (place[i], 0, 0, 0)),
            ],
        ),
        out_shape=[shape, shape],
        compiler_params=pltpu.CompilerParams(vmem_limit_bytes=32 << 20),
        cost_estimate=pl.CostEstimate(
            flops=count * 2 * PAIR * 3 * PAIR * depth,
            bytes_accessed=count * (3 * depth * PAIR * 2 + 10 * BW * BW * 2),
            transcendentals=0,
        ),
    )(owners, jnp.array(places, jnp.int32), core, flat, flat, flat)


def pack_kernel(where_ref, upper_ref, lower_ref, out_ref):
    core = where_ref[0]
    z = where_ref[1]
    for mine in range(2):

        @pl.when(core == mine)
        def _():
            for row in range(2):
                tiles = PANEL[(mine, row)][0]
                for place in range(BAND):
                    if place >= len(tiles):
                        value = jnp.zeros((BW, BW), F32)
                    elif tiles[place] < BAND:
                        value = upper_ref[tiles[place]]
                    elif mine == 1 and tiles[place] == BAND:
                        value = upper_ref[1].T
                    else:
                        value = lower_ref[tiles[place] - BAND].astype(F32).T
                    for half in range(2):
                        step = lax.rem(row * 2 + half - z + 4, 4)
                        out_ref[step, place] = value[half * 64 : (half + 1) * 64]


def pack(where, upper, lower):
    return pl.pallas_call(
        pack_kernel,
        grid_spec=pltpu.PrefetchScalarGridSpec(
            num_scalar_prefetch=1,
            grid=(1,),
            in_specs=[
                pl.BlockSpec((BAND, BW, BW), lambda i, where: (0, 0, 0)),
                pl.BlockSpec((BAND - 1, BW, BW), lambda i, where: (0, 0, 0)),
            ],
            out_specs=pl.BlockSpec((4, BAND, 64, BW), lambda i, where: (0, 0, 0, 0)),
        ),
        out_shape=jax.ShapeDtypeStruct((4, BAND, 64, BW), F32),
    )(where, upper, lower)


def split_kernel(where_ref, own_ref, first_ref, second_ref, third_ref, out_ref):
    total = (own_ref[0] + first_ref[...]) + (second_ref[...] + third_ref[...])
    core = where_ref[0]
    for mine in range(2):

        @pl.when(core == mine)
        def _():
            out_ref[0] = total[:, 32 * mine : 32 * mine + 32]
            out_ref[1] = total[:, 32 - 32 * mine : 64 - 32 * mine]


def split(where, packed, received):
    part = pl.BlockSpec((BAND, 64, BW), lambda i, where: (0, 0, 0))
    return pl.pallas_call(
        split_kernel,
        grid_spec=pltpu.PrefetchScalarGridSpec(
            num_scalar_prefetch=1,
            grid=(1,),
            in_specs=[
                pl.BlockSpec((1, BAND, 64, BW), lambda i, where: (0, 0, 0, 0)),
                part,
                part,
                part,
            ],
            out_specs=pl.BlockSpec((2, BAND, 32, BW), lambda i, where: (0, 0, 0, 0)),
        ),
        out_shape=jax.ShapeDtypeStruct((2, BAND, 32, BW), F32),
    )(where, packed, *received)


def final_kernel(where_ref, size_ref, screen_ref, own_ref, other_ref, out_ref, *, factor):
    core = where_ref[0]
    z = where_ref[1]
    owner = where_ref[2]
    for row in range(2):
        for mine in range(2):

            @pl.when(jnp.logical_and(core == mine, z // 2 == row))
            def _():
                block = owner * 2 + row
                start = (z % 2) * 64 + mine * 32
                rows = lax.broadcasted_iota(jnp.int32, (32, BW), 0) + start
                columns = lax.broadcasted_iota(jnp.int32, (32, BW), 1)
                row_mask = rows < size_ref[block]
                for half in range(2):
                    source = own_ref if half == mine else other_ref
                    for place, slot in enumerate(PANEL[(half, row)][1]):
                        offset = slot - (BAND - 1)
                        partner = jnp.clip(block + offset, 0, NB - 1)
                        first = jnp.minimum(block, partner)
                        inside = jnp.logical_and(block + offset >= 0, block + offset < NB)
                        kept = jnp.where(inside, screen_ref[first, abs(offset)], 0)
                        limit = jnp.where(kept > 0, size_ref[partner], 0)
                        mask = jnp.logical_and(row_mask, columns < limit)
                        value = source[place] if half != mine else source[0, place]
                        out_ref[:, slot * BW : (slot + 1) * BW] = jnp.where(mask, value * factor, 0.0)


def final(where, block_size, screen, pieces, other):
    factor = 1.0 / math.sqrt(AUX * OCC)
    return pl.pallas_call(
        functools.partial(final_kernel, factor=factor),
        grid_spec=pltpu.PrefetchScalarGridSpec(
            num_scalar_prefetch=3,
            grid=(1,),
            in_specs=[
                pl.BlockSpec((1, BAND, 32, BW), lambda i, *scalars: (0, 0, 0, 0)),
                pl.BlockSpec((BAND, 32, BW), lambda i, *scalars: (0, 0, 0)),
            ],
            out_specs=pl.BlockSpec((32, (2 * BAND - 1) * BW), lambda i, *scalars: (0, 0)),
        ),
        out_shape=jax.ShapeDtypeStruct((32, (2 * BAND - 1) * BW), F32),
    )(where, block_size, screen, pieces, other)


def local(three_index, block_size, screen):
    aux = lax.axis_index("aux")
    bas = lax.axis_index("bas")
    z, core = aux // 2, aux % 2
    y, x = bas // 4, bas % 4
    where = jnp.stack([core, z, bas]).astype(jnp.int32)
    flat = three_index.reshape(-1, three_index.shape[2])

    kept, received = {}, {}
    for group in GROUPS:
        pairs = jnp.array(group, jnp.int32)
        dy = jnp.where(core == 0, pairs[:, 0], pairs[:, 1])
        dx = jnp.where(core == 0, pairs[:, 1], pairs[:, 0])
        owners = ((y + dy) % 4) * 4 + (x + dx) % 4
        places = [group.index((second, first)) for first, second in group]
        mine, theirs = partial_tiles(flat, owners, places, where[:1])
        other = send(theirs, core_pairs())
        for index, key in enumerate(group):
            kept[key] = mine[index]
            received[key] = other[index]

    def chunk(step):
        own = jnp.stack([kept[(step, other)] for other in range(4)])
        other = jnp.stack([received[(step, other)] for other in range(4)])
        return own.astype(F32) + other.astype(F32)

    arrived = [send(chunk(step).astype(BF16), plane_pairs(step, True)) for step in (1, 3, 2)]
    total = chunk(0)
    for piece in arrived:
        total = total + piece.astype(F32)
    arrived = [send(total[step].astype(BF16), plane_pairs(step, False)) for step in (1, 3, 2)]
    upper = total[0]
    for piece in arrived:
        upper = upper + piece.astype(F32)

    lower = send(upper[1:].astype(BF16), mirror_pairs())
    packed = pack(where, upper, lower)
    arrived = [send(packed[step], z_pairs(step)) for step in (1, 3, 2)]
    pieces = split(where, packed, arrived)
    other = send(pieces[1], core_pairs())
    return final(where, block_size, screen, pieces, other)


def solution(mesh):
    in_specs = (P(("aux", "bas"), None, None), P(), P())
    out_specs = P(("bas", "aux"), None)
    return jax.shard_map(local, mesh=mesh, in_specs=in_specs, out_specs=out_specs, check_vma=False)
```

```python
import functools
import math

import jax
import jax.numpy as jnp
from jax import lax
from jax.experimental import pallas as pl
from jax.experimental.pallas import tpu as pltpu
from jax.sharding import PartitionSpec as P

AUX = 6144
OCC = 32
BW = 128
BAND = 5
NB = 32
OWNERS = 16
PAIR = 2 * BW
AXES = ("aux", "bas")
F32 = jnp.float32
BF16 = jnp.bfloat16

TILES = (
    ((0, 0), (0, 2), (0, 3), (1, 1), (1, 2)),
    ((1, 0), (0, 1), (0, 4), (1, 3), (1, 4)),
)
PANEL = {
    (0, 0): ((0, 1, 2, 5, 7), (4, 6, 7, 2, 3)),
    (1, 0): ((1, 2, 6, 7), (5, 8, 0, 1)),
    (0, 1): ((3, 4, 6, 8), (5, 6, 1, 2)),
    (1, 1): ((0, 3, 4, 5, 8), (4, 7, 8, 3, 0)),
}
STEPS = (2, 1, 3, 0)


def device(z, c, y, x):
    return (z * 2 + c) * 16 + y * 4 + x


EVERY = [(z, c, y, x) for z in range(4) for c in range(2) for y in range(4) for x in range(4)]


def core_pairs():
    return [(device(z, c, y, x), device(z, 1 - c, y, x)) for z, c, y, x in EVERY]


def plane_pairs(step, first):
    pairs = []
    for z, c, y, x in EVERY:
        if (c == 0) == first:
            target = device(z, c, (y + step) % 4, x)
        else:
            target = device(z, c, y, (x + step) % 4)
        pairs.append((device(z, c, y, x), target))
    return pairs


def mirror_pairs():
    pairs = []
    for z, c, y, x in EVERY:
        owner = (y * 4 + x + 1 + c) % OWNERS
        pairs.append((device(z, c, y, x), device(z, c, owner // 4, owner % 4)))
    return pairs


def z_pairs(step):
    return [(device(z, c, y, x), device((z + step) % 4, c, y, x)) for z, c, y, x in EVERY]


def send(value, pairs):
    return lax.ppermute(value, AXES, pairs)


def place_here():
    aux = lax.axis_index("aux")
    bas = lax.axis_index("bas")
    return aux // 2, aux % 2, bas


def panel(ref, block, depth):
    return ref[depth, pl.ds(pl.multiple_of(block * PAIR, PAIR), PAIR)]


def gram(left, right):
    return lax.dot_general(left, right, (((0,), (0,)), ((), ())), preferred_element_type=F32)


def set_products(flat_ref, step, bas, depth):
    y, x = bas // 4, bas % 4
    for other in range(4):
        owner = ((y + step) % 4) * 4 + (x + other) % 4
        left = panel(flat_ref, owner, depth)
        right = panel(flat_ref, jnp.minimum(owner + 1, OWNERS - 1), depth)
        zero = gram(left[:, :BW], left[:, :BW]), gram(left, right)
        owner = ((y + other) % 4) * 4 + (x + step) % 4
        left = panel(flat_ref, owner, depth)
        right = panel(flat_ref, jnp.minimum(owner + 2, OWNERS - 1), depth)
        yield zero + (gram(left, left), gram(left, right))


def put_tiles(parts, position, core, mine_ref, theirs_ref):
    low, high = slice(0, BW), slice(BW, PAIR)
    diagonal, near, block, far = parts
    zero = diagonal, near[low, low], near[low, high], near[high, low], near[high, high]
    one = block[high, high], block[low, high], far[low, low], far[high, low], far[high, high]
    for place in range(BAND):
        first, second = zero[place].astype(BF16), one[place].astype(BF16)
        mine_ref[position, place] = jnp.where(core == 0, first, second)
        theirs_ref[0, place] = jnp.where(core == 0, second, first)


def depth_parts(depth):
    sizes = (depth // 3, depth // 3, depth // 6, depth // 6)
    return [pl.ds(sum(sizes[:index]), size) for index, size in enumerate(sizes)]


def first_kernel(flat_hbm, mine_ref, theirs_ref, flat_ref, small_ref, sums_ref, sems, *, step):
    z, core, bas = place_here()
    depths = depth_parts(flat_ref.shape[0])
    copies = [
        pltpu.make_async_copy(flat_hbm.at[depth], flat_ref.at[depth], sems.at[index])
        for index, depth in enumerate(depths)
    ]
    for copy in copies:
        copy.start()
    for index, (copy, depth) in enumerate(zip(copies, depths)):
        copy.wait()
        for position, parts in enumerate(set_products(flat_ref, step, bas, depth)):
            if index > 0:
                before = (small_ref[position], *(sums_ref[position, place] for place in range(3)))
                parts = [total + part for total, part in zip(before, parts)]
            if index < len(depths) - 1:
                small_ref[position] = parts[0]
                for place, part in enumerate(parts[1:]):
                    sums_ref[position, place] = part
            else:
                put_tiles(parts, position, core, mine_ref, theirs_ref.at[pl.ds(position, 1)])


def later_kernel(flat_ref, after_ref, mine_ref, *theirs_refs, step):
    z, core, bas = place_here()
    for position, parts in enumerate(set_products(flat_ref, step, bas, pl.ds(0, flat_ref.shape[0]))):
        size = 4 // len(theirs_refs)
        theirs_ref = theirs_refs[position // size].at[pl.ds(position % size, 1)]
        put_tiles(parts, position, core, mine_ref, theirs_ref)


VMEM = pl.BlockSpec(memory_space=pltpu.VMEM)
ANYWHERE = pl.BlockSpec(memory_space=pl.ANY)
SMALL = pltpu.CompilerParams(vmem_limit_bytes=4 << 20)
SCALARS = pl.BlockSpec(memory_space=pltpu.SMEM)


SET = jax.ShapeDtypeStruct((4, BAND, BW, BW), BF16)


def cost(depth, moved=0):
    return pl.CostEstimate(
        flops=4 * 13 * PAIR * PAIR * depth // 2, bytes_accessed=moved, transcendentals=0
    )


def first_tiles(flat, step):
    depth = flat.shape[0]
    return pl.pallas_call(
        functools.partial(first_kernel, step=step),
        in_specs=[ANYWHERE],
        out_specs=[VMEM, VMEM, VMEM],
        out_shape=[SET, SET, pltpu.VMEM(flat.shape, BF16)],
        scratch_shapes=[
            pltpu.VMEM((4, BW, BW), F32),
            pltpu.VMEM((4, 3, PAIR, PAIR), F32),
            pltpu.SemaphoreType.DMA((4,)),
        ],
        compiler_params=pltpu.CompilerParams(vmem_limit_bytes=20 << 20),
        cost_estimate=cost(depth, flat.size * 2),
    )(pltpu.with_memory_space_constraint(flat, pltpu.HBM))


def later_tiles(flat, after, step, pieces=1):
    return pl.pallas_call(
        functools.partial(later_kernel, step=step),
        in_specs=[VMEM, ANYWHERE],
        out_specs=[VMEM] * (1 + pieces),
        out_shape=[SET] + [jax.ShapeDtypeStruct((4 // pieces, BAND, BW, BW), BF16)] * pieces,
        compiler_params=pltpu.CompilerParams(vmem_limit_bytes=16 << 20),
        cost_estimate=cost(flat.shape[0]),
    )(flat, after)


def total_kernel(*refs):
    mine_ref, other_ref, *arrived, own_ref, first_ref, second_ref, third_ref = refs
    for position, out_ref in enumerate((own_ref, first_ref, second_ref, third_ref)):
        total = mine_ref[position].astype(F32) + other_ref[position].astype(F32)
        for ref in arrived:
            total = total + ref[position].astype(F32)
        out_ref[...] = total.astype(out_ref.dtype)


def first_total(mine, other, arrived):
    sent = jax.ShapeDtypeStruct((BAND, BW, BW), BF16)
    return pl.pallas_call(
        total_kernel,
        in_specs=[VMEM] * 5,
        out_specs=[VMEM] * 4,
        out_shape=[jax.ShapeDtypeStruct((BAND, BW, BW), F32), sent, sent, sent],
        compiler_params=SMALL,
    )(mine, other, *arrived)


def pair_sum(mine, other):
    return (mine.astype(F32) + other.astype(F32)).astype(BF16)


def pack_kernel(upper_ref, lower_ref, own_ref, *sent_refs):
    z, core, _ = place_here()
    for mine in range(2):
        for row in range(2):
            tiles = PANEL[(mine, row)][0]
            for half in range(2):
                target = row * 2 + half
                rows = pl.ds(half * 64, 64)

                def value(index):
                    if index < BAND:
                        return upper_ref[index, rows]
                    if mine == 1 and index == BAND:
                        return upper_ref[1, :, rows].T
                    return lower_ref[index - BAND, :, rows].astype(F32).T

                @pl.when(jnp.logical_and(core == mine, z == target))
                def _():
                    for place, index in enumerate(tiles):
                        own_ref[place] = value(index)
                    if len(tiles) < BAND:
                        own_ref[BAND - 1] = jnp.zeros((64, BW), F32)

                for step in range(1, 4):

                    @pl.when(jnp.logical_and(core == mine, (z + step) % 4 == target))
                    def _():
                        out_ref = sent_refs[step - 1]
                        rest = jnp.zeros((64, BW), BF16)
                        for place, index in enumerate(tiles):
                            whole = value(index)
                            high = whole.astype(BF16)
                            out_ref[place] = high
                            if index == 0:
                                rest = (whole - high.astype(F32)).astype(BF16)
                        if len(tiles) < BAND:
                            out_ref[BAND - 1] = jnp.zeros((64, BW), BF16)
                        out_ref[BAND] = rest


def pack(upper, lower):
    own = jax.ShapeDtypeStruct((BAND, 64, BW), F32)
    sent = jax.ShapeDtypeStruct((BAND + 1, 64, BW), BF16)
    return pl.pallas_call(
        pack_kernel,
        in_specs=[VMEM, VMEM],
        out_specs=[VMEM] * 4,
        out_shape=[own] + [sent] * 3,
        compiler_params=SMALL,
    )(upper, lower)


def split_kernel(own_ref, first_ref, second_ref, third_ref, kept_ref, sent_ref):
    z, core, _ = place_here()
    for ref, part in ((kept_ref, core), (sent_ref, 1 - core)):
        rows = pl.ds(pl.multiple_of(part * 32, 32), 32)
        for place in range(BAND):
            total = own_ref[place, rows]
            for source in (first_ref, second_ref, third_ref):
                total = total + source[place, rows].astype(F32)
                if place == 0:
                    total = total + source[BAND, rows].astype(F32)
            ref[place] = total


def split(own, arrived):
    shape = jax.ShapeDtypeStruct((BAND, 32, BW), F32)
    return pl.pallas_call(
        split_kernel,
        in_specs=[VMEM] * 4,
        out_specs=[VMEM] * 2,
        out_shape=[shape] * 2,
        compiler_params=SMALL,
    )(own, *arrived)


def final_kernel(size_ref, screen_ref, own_ref, other_ref, out_ref, *, factor):
    z, core, owner = place_here()
    for row in range(2):
        for mine in range(2):

            @pl.when(jnp.logical_and(core == mine, z // 2 == row))
            def _():
                block = owner * 2 + row
                start = (z % 2) * 64 + mine * 32
                rows = lax.broadcasted_iota(jnp.int32, (32, BW), 0) + start
                columns = lax.broadcasted_iota(jnp.int32, (32, BW), 1)
                row_mask = rows < size_ref[block]
                for half in range(2):
                    source = own_ref if half == mine else other_ref
                    for place, slot in enumerate(PANEL[(half, row)][1]):
                        offset = slot - (BAND - 1)
                        partner = jnp.clip(block + offset, 0, NB - 1)
                        inside = jnp.logical_and(block + offset >= 0, block + offset < NB)
                        kept = jnp.where(inside, screen_ref[abs(offset), jnp.minimum(block, partner)], 0)
                        limit = jnp.where(kept > 0, size_ref[partner], 0)
                        mask = jnp.logical_and(row_mask, columns < limit)
                        out_ref[:, slot * BW : (slot + 1) * BW] = jnp.where(mask, source[place] * factor, 0.0)


def final(block_size, screen, own, other):
    factor = 1.0 / math.sqrt(AUX * OCC)
    return pl.pallas_call(
        functools.partial(final_kernel, factor=factor),
        in_specs=[SCALARS, SCALARS, VMEM, VMEM],
        out_specs=VMEM,
        out_shape=jax.ShapeDtypeStruct((32, (2 * BAND - 1) * BW), F32),
        compiler_params=SMALL,
    )(block_size, screen.T, own, other)


def local(three_index, block_size, screen):
    flat = three_index.reshape(-1, three_index.shape[2])
    def exchanged(pieces):
        return jnp.concatenate([send(piece, core_pairs()) for piece in pieces])

    def passed(step, mine, other):
        outgoing = pair_sum(mine, other)
        return outgoing, send(outgoing, plane_pairs(step, True))

    mine, theirs, held = first_tiles(flat, STEPS[0])
    other = send(theirs, core_pairs())
    next_mine, *next_theirs = later_tiles(held, block_size, STEPS[1], 1)
    next_other = exchanged(next_theirs)
    sent1, arrived1 = passed(STEPS[0], mine, other)
    sent2, arrived2 = passed(STEPS[1], next_mine, next_other)
    mine, *theirs = later_tiles(held, sent2, STEPS[2], 2)
    other = exchanged(theirs)
    sent3, arrived3 = passed(STEPS[2], mine, other)
    mine, *theirs = later_tiles(held, arrived1, STEPS[3], 1)
    upper, *outgoing = first_total(mine, exchanged(theirs), [arrived1, arrived2, arrived3])
    arrived = [send(outgoing[step - 1], plane_pairs(step, False)) for step in (2, 1, 3)]
    for piece in arrived:
        upper = upper + piece.astype(F32)

    lower = send(upper[1:].astype(BF16), mirror_pairs())
    own, *outgoing = pack(upper, lower)
    arrived = [send(outgoing[step - 1], z_pairs(step)) for step in (2, 1, 3)]
    own, theirs = split(own, arrived)
    other = send(theirs, core_pairs())
    return final(block_size, screen, own, other)


def solution(mesh):
    in_specs = (P(("aux", "bas"), None, None), P(), P())
    out_specs = P(("bas", "aux"), None)
    return jax.shard_map(local, mesh=mesh, in_specs=in_specs, out_specs=out_specs, check_vma=False)
```

```python
import functools
import math

import jax
import jax.numpy as jnp
from jax import lax
from jax.experimental import pallas as pl
from jax.experimental.pallas import tpu as pltpu
from jax.sharding import PartitionSpec as P

AUX = 6144
OCC = 32
BW = 128
BAND = 5
NB = 32
OWNERS = 16
PAIR = 2 * BW
AXES = ("aux", "bas")
F32 = jnp.float32
BF16 = jnp.bfloat16

TILES = (
    ((0, 0), (0, 2), (0, 3), (1, 1), (1, 2)),
    ((1, 0), (0, 1), (0, 4), (1, 3), (1, 4)),
)
MIRROR = BAND
UPPER = {(0, 0): (0, 1, 2), (1, 0): (1, 2), (0, 1): (3, 4), (1, 1): (0, 3, 4, MIRROR)}
LOWER = {(0, 0): (1, 3), (1, 0): (2, 3), (0, 1): (2, 4), (1, 1): (4,)}
SLOTS = {(0, 0): (4, 6, 7, 2, 3), (1, 0): (5, 8, 0, 1), (0, 1): (5, 6, 1, 2), (1, 1): (4, 7, 8, 3, 0)}
SLOT_COUNT = 2 * BAND - 1
STEPS = (2, 1, 3, 0)


def device(z, c, y, x):
    return (z * 2 + c) * 16 + y * 4 + x


EVERY = [(z, c, y, x) for z in range(4) for c in range(2) for y in range(4) for x in range(4)]


def core_pairs():
    return [(device(z, c, y, x), device(z, 1 - c, y, x)) for z, c, y, x in EVERY]


def plane_pairs(step, first):
    pairs = []
    for z, c, y, x in EVERY:
        if (c == 0) == first:
            target = device(z, c, (y + step) % 4, x)
        else:
            target = device(z, c, y, (x + step) % 4)
        pairs.append((device(z, c, y, x), target))
    return pairs


def mirror_pairs():
    pairs = []
    for z, c, y, x in EVERY:
        owner = (y * 4 + x + 1 + c) % OWNERS
        pairs.append((device(z, c, y, x), device(z, c, owner // 4, owner % 4)))
    return pairs


def z_pairs(step):
    return [(device(z, c, y, x), device((z + step) % 4, c, y, x)) for z, c, y, x in EVERY]


def send(value, pairs):
    return lax.ppermute(value, AXES, pairs)


def place_here():
    aux = lax.axis_index("aux")
    bas = lax.axis_index("bas")
    return aux // 2, aux % 2, bas


def panel(ref, block, depth):
    return ref[depth, pl.ds(pl.multiple_of(block * PAIR, PAIR), PAIR)]


def gram(left, right):
    return lax.dot_general(left, right, (((0,), (0,)), ((), ())), preferred_element_type=F32)


def set_products(flat_ref, step, bas, depth):
    y, x = bas // 4, bas % 4
    for other in range(4):
        owner = ((y + step) % 4) * 4 + (x + other) % 4
        left = panel(flat_ref, owner, depth)
        right = panel(flat_ref, jnp.minimum(owner + 1, OWNERS - 1), depth)
        zero = gram(left[:, :BW], left[:, :BW]), gram(left, right)
        owner = ((y + other) % 4) * 4 + (x + step) % 4
        left = panel(flat_ref, owner, depth)
        right = panel(flat_ref, jnp.minimum(owner + 2, OWNERS - 1), depth)
        yield zero + (gram(left, left), gram(left, right))


def put_tiles(parts, position, core, mine_ref, theirs_ref):
    low, high = slice(0, BW), slice(BW, PAIR)
    diagonal, near, block, far = parts
    zero = diagonal, near[low, low], near[low, high], near[high, low], near[high, high]
    one = block[high, high], block[low, high], far[low, low], far[high, low], far[high, high]
    for place in range(BAND):
        first, second = zero[place].astype(BF16), one[place].astype(BF16)
        mine_ref[position, place] = jnp.where(core == 0, first, second)
        theirs_ref[0, place] = jnp.where(core == 0, second, first)


def depth_parts(depth):
    sizes = (depth // 3, depth // 3, depth // 6, depth // 6)
    return [pl.ds(sum(sizes[:index]), size) for index, size in enumerate(sizes)]


def first_kernel(flat_hbm, mine_ref, theirs_ref, flat_ref, small_ref, sums_ref, sems, *, step):
    z, core, bas = place_here()
    depths = depth_parts(flat_ref.shape[0])
    copies = [
        pltpu.make_async_copy(flat_hbm.at[depth], flat_ref.at[depth], sems.at[index])
        for index, depth in enumerate(depths)
    ]
    for copy in copies:
        copy.start()
    for index, (copy, depth) in enumerate(zip(copies, depths)):
        copy.wait()
        for position, parts in enumerate(set_products(flat_ref, step, bas, depth)):
            if index > 0:
                before = (small_ref[position], *(sums_ref[position, place] for place in range(3)))
                parts = [total + part for total, part in zip(before, parts)]
            if index < len(depths) - 1:
                small_ref[position] = parts[0]
                for place, part in enumerate(parts[1:]):
                    sums_ref[position, place] = part
            else:
                put_tiles(parts, position, core, mine_ref, theirs_ref.at[pl.ds(position, 1)])


def later_kernel(flat_ref, after_ref, mine_ref, *theirs_refs, step):
    z, core, bas = place_here()
    for position, parts in enumerate(set_products(flat_ref, step, bas, pl.ds(0, flat_ref.shape[0]))):
        size = 4 // len(theirs_refs)
        theirs_ref = theirs_refs[position // size].at[pl.ds(position % size, 1)]
        put_tiles(parts, position, core, mine_ref, theirs_ref)


def last_kernel(size_ref, screen_ref, flat_ref, after_ref, mine_ref, theirs_ref, mask_ref, *, step, factor):
    later_kernel(flat_ref, after_ref, mine_ref, theirs_ref, step=step)
    z, core, bas = place_here()
    block = bas * 2 + z // 2
    rows = lax.broadcasted_iota(jnp.int32, (32, BW), 0) + (z % 2) * 64 + core * 32
    columns = lax.broadcasted_iota(jnp.int32, (32, BW), 1)
    row_mask = rows < size_ref[block]
    for slot in range(SLOT_COUNT):
        offset = slot - (BAND - 1)
        partner = jnp.clip(block + offset, 0, NB - 1)
        inside = jnp.logical_and(block + offset >= 0, block + offset < NB)
        kept = jnp.where(inside, screen_ref[abs(offset), jnp.minimum(block, partner)], 0)
        limit = jnp.where(kept > 0, size_ref[partner], 0)
        mask = jnp.logical_and(row_mask, columns < limit)
        mask_ref[:, slot * BW : (slot + 1) * BW] = jnp.where(mask, factor, 0.0)


VMEM = pl.BlockSpec(memory_space=pltpu.VMEM)
ANYWHERE = pl.BlockSpec(memory_space=pl.ANY)
SMALL = pltpu.CompilerParams(vmem_limit_bytes=4 << 20)
SCALARS = pl.BlockSpec(memory_space=pltpu.SMEM)


SET = jax.ShapeDtypeStruct((4, BAND, BW, BW), BF16)


def cost(depth, moved=0):
    return pl.CostEstimate(
        flops=4 * 13 * PAIR * PAIR * depth // 2, bytes_accessed=moved, transcendentals=0
    )


def first_tiles(flat, step):
    depth = flat.shape[0]
    return pl.pallas_call(
        functools.partial(first_kernel, step=step),
        in_specs=[ANYWHERE],
        out_specs=[VMEM, VMEM, VMEM],
        out_shape=[SET, SET, pltpu.VMEM(flat.shape, BF16)],
        scratch_shapes=[
            pltpu.VMEM((4, BW, BW), F32),
            pltpu.VMEM((4, 3, PAIR, PAIR), F32),
            pltpu.SemaphoreType.DMA((4,)),
        ],
        compiler_params=pltpu.CompilerParams(vmem_limit_bytes=20 << 20),
        cost_estimate=cost(depth, flat.size * 2),
    )(pltpu.with_memory_space_constraint(flat, pltpu.HBM))


def later_tiles(flat, after, step, pieces=1):
    return pl.pallas_call(
        functools.partial(later_kernel, step=step),
        in_specs=[VMEM, ANYWHERE],
        out_specs=[VMEM] * (1 + pieces),
        out_shape=[SET] + [jax.ShapeDtypeStruct((4 // pieces, BAND, BW, BW), BF16)] * pieces,
        compiler_params=pltpu.CompilerParams(vmem_limit_bytes=16 << 20),
        cost_estimate=cost(flat.shape[0]),
    )(flat, after)


def last_tiles(block_size, screen, flat, after, step):
    factor = 1.0 / math.sqrt(AUX * OCC)
    return pl.pallas_call(
        functools.partial(last_kernel, step=step, factor=factor),
        in_specs=[SCALARS, SCALARS, VMEM, ANYWHERE],
        out_specs=[VMEM] * 3,
        out_shape=[SET, SET, jax.ShapeDtypeStruct((32, SLOT_COUNT * BW), F32)],
        compiler_params=pltpu.CompilerParams(vmem_limit_bytes=16 << 20),
        cost_estimate=cost(flat.shape[0]),
    )(block_size, screen.T, flat, after)


def total_kernel(*refs):
    mine_ref, other_ref, *arrived, own_ref, first_ref, second_ref, third_ref = refs
    for position, out_ref in enumerate((own_ref, first_ref, second_ref, third_ref)):
        total = mine_ref[position].astype(F32) + other_ref[position].astype(F32)
        for ref in arrived:
            total = total + ref[position].astype(F32)
        out_ref[...] = total.astype(out_ref.dtype)


def first_total(mine, other, arrived):
    sent = jax.ShapeDtypeStruct((BAND, BW, BW), BF16)
    return pl.pallas_call(
        total_kernel,
        in_specs=[VMEM] * 5,
        out_specs=[VMEM] * 4,
        out_shape=[jax.ShapeDtypeStruct((BAND, BW, BW), F32), sent, sent, sent],
        compiler_params=SMALL,
    )(mine, other, *arrived)


def pair_sum(mine, other):
    return (mine.astype(F32) + other.astype(F32)).astype(BF16)


def pack_kernel(own_ref, first_ref, second_ref, third_ref, kept_ref, turned_ref, *refs):
    upper_refs, sums_ref, mirror_ref = refs[:3], refs[3], refs[4]
    z, core, _ = place_here()
    for index in range(BAND):
        total = own_ref[index]
        for ref in (first_ref, second_ref, third_ref):
            total = total + ref[index].astype(F32)
        sums_ref[index] = total
        if index > 0:
            turned = total.T
            turned_ref[index - 1] = turned.astype(BF16)
            if index == 1:
                mirror_ref[...] = turned
    for mine in range(2):
        for row in range(2):
            for half in range(2):
                target = row * 2 + half
                rows = pl.ds(half * 64, 64)
                upper = UPPER[(mine, row)]

                def value(index):
                    return mirror_ref[rows] if index == MIRROR else sums_ref[index, rows]

                @pl.when(jnp.logical_and(core == mine, z == target))
                def _():
                    for place, index in enumerate(upper):
                        kept_ref[place] = value(index)

                for step in range(1, 4):

                    @pl.when(jnp.logical_and(core == mine, (z + step) % 4 == target))
                    def _():
                        out_ref = upper_refs[step - 1]
                        for place in range(BAND):
                            out_ref[place] = jnp.zeros((64, BW), BF16)
                        for place, index in enumerate(upper):
                            whole = value(index)
                            high = whole.astype(BF16)
                            out_ref[place] = high
                            if index == 0:
                                out_ref[BAND - 1] = (whole - high.astype(F32)).astype(BF16)


def pack(own, arrived):
    kept = jax.ShapeDtypeStruct((BAND - 1, 64, BW), F32)
    turned = jax.ShapeDtypeStruct((BAND - 1, BW, BW), BF16)
    upper = jax.ShapeDtypeStruct((BAND, 64, BW), BF16)
    return pl.pallas_call(
        pack_kernel,
        in_specs=[VMEM] * 4,
        out_specs=[VMEM] * 5,
        out_shape=[kept, turned] + [upper] * 3,
        scratch_shapes=[pltpu.VMEM((BAND, BW, BW), F32), pltpu.VMEM((BW, BW), F32)],
        compiler_params=SMALL,
    )(own, *arrived)


def lower_kernel(turned_ref, *out_refs):
    z, core, _ = place_here()
    for mine in range(2):
        for row in range(2):
            for half in range(2):
                for step in range(4):

                    @pl.when(jnp.logical_and(core == mine, (z + step) % 4 == row * 2 + half))
                    def _():
                        lower = LOWER[(mine, row)]
                        for place in range(2):
                            index = lower[min(place, len(lower) - 1)] - 1
                            out_refs[step][place] = turned_ref[index, half * 64 : half * 64 + 64]


def pack_lower(turned):
    lower = jax.ShapeDtypeStruct((2, 64, BW), BF16)
    return pl.pallas_call(
        lower_kernel, in_specs=[VMEM], out_specs=[VMEM] * 4, out_shape=[lower] * 4, compiler_params=SMALL
    )(turned)


def split_kernel(own_ref, *refs):
    upper_refs, lower_refs, kept_ref, sent_ref = refs[:3], refs[3:7], refs[7], refs[8]
    z, core, _ = place_here()
    for ref, part in ((kept_ref, core), (sent_ref, 1 - core)):
        rows = pl.ds(pl.multiple_of(part * 32, 32), 32)
        for mine in range(2):
            for row in range(2):

                @pl.when(jnp.logical_and(core == mine, z // 2 == row))
                def _():
                    count = len(UPPER[(mine, row)])
                    for place in range(count):
                        total = own_ref[place, rows]
                        for source in upper_refs:
                            total = total + source[place, rows].astype(F32)
                            if UPPER[(mine, row)][place] == 0:
                                total = total + source[BAND - 1, rows].astype(F32)
                        ref[place] = total
                    for place in range(len(LOWER[(mine, row)])):
                        first, second, third, fourth = (source[place, rows].astype(F32) for source in lower_refs)
                        ref[count + place] = (first + second) + (third + fourth)
                    for place in range(len(SLOTS[(mine, row)]), BAND):
                        ref[place] = jnp.zeros((32, BW), F32)


def split(own, upper, lower):
    shape = jax.ShapeDtypeStruct((BAND, 32, BW), F32)
    return pl.pallas_call(
        split_kernel,
        in_specs=[VMEM] * 8,
        out_specs=[VMEM] * 2,
        out_shape=[shape] * 2,
        compiler_params=SMALL,
    )(own, *upper, *lower)


def final_kernel(mask_ref, own_ref, other_ref, out_ref):
    z, core, _ = place_here()
    for row in range(2):
        for mine in range(2):

            @pl.when(jnp.logical_and(core == mine, z // 2 == row))
            def _():
                for half in range(2):
                    source = own_ref if half == mine else other_ref
                    for place, slot in enumerate(SLOTS[(half, row)]):
                        columns = slice(slot * BW, (slot + 1) * BW)
                        out_ref[:, columns] = source[place] * mask_ref[:, columns]


def final(mask, own, other):
    return pl.pallas_call(
        final_kernel,
        in_specs=[VMEM] * 3,
        out_specs=VMEM,
        out_shape=jax.ShapeDtypeStruct(mask.shape, F32),
        compiler_params=SMALL,
    )(mask, own, other)


def local(three_index, block_size, screen):
    flat = three_index.reshape(-1, three_index.shape[2])
    def exchanged(pieces):
        return jnp.concatenate([send(piece, core_pairs()) for piece in pieces])

    def passed(step, mine, other):
        outgoing = pair_sum(mine, other)
        return outgoing, send(outgoing, plane_pairs(step, True))

    mine, theirs, held = first_tiles(flat, STEPS[0])
    other = send(theirs, core_pairs())
    next_mine, *next_theirs = later_tiles(held, block_size, STEPS[1], 1)
    next_other = exchanged(next_theirs)
    sent1, arrived1 = passed(STEPS[0], mine, other)
    sent2, arrived2 = passed(STEPS[1], next_mine, next_other)
    mine, *theirs = later_tiles(held, sent2, STEPS[2], 2)
    other = exchanged(theirs)
    sent3, arrived3 = passed(STEPS[2], mine, other)
    mine, theirs, mask = last_tiles(block_size, screen, held, arrived1, STEPS[3])
    own, *outgoing = first_total(mine, send(theirs, core_pairs()), [arrived1, arrived2, arrived3])
    arrived = [send(outgoing[step - 1], plane_pairs(step, False)) for step in (1, 3, 2)]
    own, turned, *outgoing = pack(own, arrived)
    turned = send(turned, mirror_pairs())
    upper = [send(outgoing[step - 1], z_pairs(step)) for step in (1, 3, 2)]
    kept, *outgoing = pack_lower(turned)
    lower = [kept] + [send(outgoing[step - 1], z_pairs(step)) for step in (1, 3, 2)]
    own, theirs = split(own, upper, lower)
    return final(mask, own, send(theirs, core_pairs()))


def solution(mesh):
    in_specs = (P(("aux", "bas"), None, None), P(), P())
    out_specs = P(("bas", "aux"), None)
    return jax.shard_map(local, mesh=mesh, in_specs=in_specs, out_specs=out_specs, check_vma=False)
```

```python
import functools
import math

import jax
import jax.numpy as jnp
from jax import lax
from jax.experimental import pallas as pl
from jax.experimental.pallas import tpu as pltpu
from jax.sharding import PartitionSpec as P

AUX = 6144
OCC = 32
BW = 128
BAND = 5
NB = 32
OWNERS = 16
PAIR = 2 * BW
AXES = ("aux", "bas")
F32 = jnp.float32
BF16 = jnp.bfloat16

TILES = (
    ((0, 0), (0, 2), (0, 3), (1, 1), (1, 2)),
    ((1, 0), (0, 1), (0, 4), (1, 3), (1, 4)),
)
MIRROR = BAND
UPPER = {(0, 0): (0, 1, 2), (1, 0): (1, 2), (0, 1): (3, 4), (1, 1): (0, 3, 4, MIRROR)}
LOWER = {(0, 0): (1, 3), (1, 0): (2, 3), (0, 1): (2, 4), (1, 1): (4,)}
SLOTS = {(0, 0): (4, 6, 7, 2, 3), (1, 0): (5, 8, 0, 1), (0, 1): (5, 6, 1, 2), (1, 1): (4, 7, 8, 3, 0)}
SLOT_COUNT = 2 * BAND - 1
STEPS = (2, 1, 3, 0)


def device(z, c, y, x):
    return (z * 2 + c) * 16 + y * 4 + x


EVERY = [(z, c, y, x) for z in range(4) for c in range(2) for y in range(4) for x in range(4)]


def core_pairs():
    return [(device(z, c, y, x), device(z, 1 - c, y, x)) for z, c, y, x in EVERY]


def plane_pairs(step, first):
    pairs = []
    for z, c, y, x in EVERY:
        if (c == 0) == first:
            target = device(z, c, (y + step) % 4, x)
        else:
            target = device(z, c, y, (x + step) % 4)
        pairs.append((device(z, c, y, x), target))
    return pairs


def mirror_pairs():
    pairs = []
    for z, c, y, x in EVERY:
        owner = (y * 4 + x + 1 + c) % OWNERS
        pairs.append((device(z, c, y, x), device(z, c, owner // 4, owner % 4)))
    return pairs


def z_pairs(step):
    return [(device(z, c, y, x), device((z + step) % 4, c, y, x)) for z, c, y, x in EVERY]


def send(value, pairs):
    return lax.ppermute(value, AXES, pairs)


def place_here():
    aux = lax.axis_index("aux")
    bas = lax.axis_index("bas")
    return aux // 2, aux % 2, bas


def panel(ref, block, depth):
    return ref[depth, pl.ds(pl.multiple_of(block * PAIR, PAIR), PAIR)]


def gram(left, right):
    return lax.dot_general(left, right, (((0,), (0,)), ((), ())), preferred_element_type=F32)


def set_products(flat_ref, step, bas, depth):
    y, x = bas // 4, bas % 4
    for other in range(4):
        owner = ((y + step) % 4) * 4 + (x + other) % 4
        left = panel(flat_ref, owner, depth)
        right = panel(flat_ref, jnp.minimum(owner + 1, OWNERS - 1), depth)
        zero = gram(left[:, :BW], left[:, :BW]), gram(left, right)
        owner = ((y + other) % 4) * 4 + (x + step) % 4
        left = panel(flat_ref, owner, depth)
        right = panel(flat_ref, jnp.minimum(owner + 2, OWNERS - 1), depth)
        yield zero + (gram(left, left), gram(left, right))


def put_tiles(parts, position, core, mine_ref, theirs_ref):
    low, high = slice(0, BW), slice(BW, PAIR)
    diagonal, near, block, far = parts
    zero = diagonal, near[low, low], near[low, high], near[high, low], near[high, high]
    one = block[high, high], block[low, high], far[low, low], far[high, low], far[high, high]
    for place in range(BAND):
        first, second = zero[place].astype(BF16), one[place].astype(BF16)
        mine_ref[position, place] = jnp.where(core == 0, first, second)
        theirs_ref[0, place] = jnp.where(core == 0, second, first)


def depth_parts(depth):
    sizes = (depth // 3, depth // 3, depth // 6, depth // 6)
    return [pl.ds(sum(sizes[:index]), size) for index, size in enumerate(sizes)]


def first_kernel(flat_hbm, mine_ref, theirs_ref, flat_ref, small_ref, sums_ref, sems, *, step):
    z, core, bas = place_here()
    depths = depth_parts(flat_ref.shape[0])
    copies = [
        pltpu.make_async_copy(flat_hbm.at[depth], flat_ref.at[depth], sems.at[index])
        for index, depth in enumerate(depths)
    ]
    for copy in copies:
        copy.start()
    for index, (copy, depth) in enumerate(zip(copies, depths)):
        copy.wait()
        for position, parts in enumerate(set_products(flat_ref, step, bas, depth)):
            if index > 0:
                before = (small_ref[position], *(sums_ref[position, place] for place in range(3)))
                parts = [total + part for total, part in zip(before, parts)]
            if index < len(depths) - 1:
                small_ref[position] = parts[0]
                for place, part in enumerate(parts[1:]):
                    sums_ref[position, place] = part
            else:
                put_tiles(parts, position, core, mine_ref, theirs_ref.at[pl.ds(position, 1)])


def later_kernel(flat_ref, after_ref, mine_ref, *theirs_refs, step):
    z, core, bas = place_here()
    for position, parts in enumerate(set_products(flat_ref, step, bas, pl.ds(0, flat_ref.shape[0]))):
        size = 4 // len(theirs_refs)
        theirs_ref = theirs_refs[position // size].at[pl.ds(position % size, 1)]
        put_tiles(parts, position, core, mine_ref, theirs_ref)


def last_kernel(size_ref, screen_ref, flat_ref, after_ref, mine_ref, theirs_ref, mask_ref, *, step, factor):
    later_kernel(flat_ref, after_ref, mine_ref, theirs_ref, step=step)
    z, core, bas = place_here()
    block = bas * 2 + z // 2
    rows = lax.broadcasted_iota(jnp.int32, (32, BW), 0) + (z % 2) * 64 + core * 32
    columns = lax.broadcasted_iota(jnp.int32, (32, BW), 1)
    row_mask = rows < size_ref[block]
    for slot in range(SLOT_COUNT):
        offset = slot - (BAND - 1)
        partner = jnp.clip(block + offset, 0, NB - 1)
        inside = jnp.logical_and(block + offset >= 0, block + offset < NB)
        kept = jnp.where(inside, screen_ref[abs(offset), jnp.minimum(block, partner)], 0)
        limit = jnp.where(kept > 0, size_ref[partner], 0)
        mask = jnp.logical_and(row_mask, columns < limit)
        mask_ref[:, slot * BW : (slot + 1) * BW] = jnp.where(mask, factor, 0.0)


VMEM = pl.BlockSpec(memory_space=pltpu.VMEM)
ANYWHERE = pl.BlockSpec(memory_space=pl.ANY)
SMALL = pltpu.CompilerParams(vmem_limit_bytes=4 << 20)
SCALARS = pl.BlockSpec(memory_space=pltpu.SMEM)


SET = jax.ShapeDtypeStruct((4, BAND, BW, BW), BF16)


def cost(depth, moved=0):
    return pl.CostEstimate(
        flops=4 * 13 * PAIR * PAIR * depth // 2, bytes_accessed=moved, transcendentals=0
    )


def first_tiles(flat, step):
    depth = flat.shape[0]
    return pl.pallas_call(
        functools.partial(first_kernel, step=step),
        in_specs=[ANYWHERE],
        out_specs=[VMEM, VMEM, VMEM],
        out_shape=[SET, SET, pltpu.VMEM(flat.shape, BF16)],
        scratch_shapes=[
            pltpu.VMEM((4, BW, BW), F32),
            pltpu.VMEM((4, 3, PAIR, PAIR), F32),
            pltpu.SemaphoreType.DMA((4,)),
        ],
        compiler_params=pltpu.CompilerParams(vmem_limit_bytes=20 << 20),
        cost_estimate=cost(depth, flat.size * 2),
    )(pltpu.with_memory_space_constraint(flat, pltpu.HBM))


def later_tiles(flat, after, step, pieces=1):
    return pl.pallas_call(
        functools.partial(later_kernel, step=step),
        in_specs=[VMEM, ANYWHERE],
        out_specs=[VMEM] * (1 + pieces),
        out_shape=[SET] + [jax.ShapeDtypeStruct((4 // pieces, BAND, BW, BW), BF16)] * pieces,
        compiler_params=pltpu.CompilerParams(vmem_limit_bytes=16 << 20),
        cost_estimate=cost(flat.shape[0]),
    )(flat, after)


def last_tiles(block_size, screen, flat, after, step):
    factor = 1.0 / math.sqrt(AUX * OCC)
    return pl.pallas_call(
        functools.partial(last_kernel, step=step, factor=factor),
        in_specs=[SCALARS, SCALARS, VMEM, ANYWHERE],
        out_specs=[VMEM] * 3,
        out_shape=[SET, SET, jax.ShapeDtypeStruct((32, SLOT_COUNT * BW), F32)],
        compiler_params=pltpu.CompilerParams(vmem_limit_bytes=16 << 20),
        cost_estimate=cost(flat.shape[0]),
    )(block_size, screen.T, flat, after)


def total_kernel(*refs):
    mine_ref, other_ref, *arrived, own_ref, first_ref, second_ref, third_ref = refs
    for position, out_ref in enumerate((own_ref, first_ref, second_ref, third_ref)):
        total = mine_ref[position].astype(F32) + other_ref[position].astype(F32)
        for ref in arrived:
            total = total + ref[position].astype(F32)
        out_ref[...] = total.astype(out_ref.dtype)


def first_total(mine, other, arrived):
    sent = jax.ShapeDtypeStruct((BAND, BW, BW), BF16)
    return pl.pallas_call(
        total_kernel,
        in_specs=[VMEM] * 5,
        out_specs=[VMEM] * 4,
        out_shape=[jax.ShapeDtypeStruct((BAND, BW, BW), F32), sent, sent, sent],
        compiler_params=SMALL,
    )(mine, other, *arrived)


def pair_sum(mine, other):
    return (mine.astype(F32) + other.astype(F32)).astype(BF16)


def pack_kernel(own_ref, first_ref, second_ref, third_ref, upper_ref, lower_ref, *refs):
    out_refs, sums_ref, turned_ref = refs[:3], refs[3], refs[4]
    z, core, _ = place_here()
    for index in range(BAND):
        total = own_ref[index]
        for ref in (first_ref, second_ref, third_ref):
            total = total + ref[index].astype(F32)
        sums_ref[index] = total
        if index > 0:
            turned_ref[index] = total.T
    for mine in range(2):
        for row in range(2):
            for half in range(2):
                target = row * 2 + half
                rows = pl.ds(half * 64, 64)
                upper, lower = UPPER[(mine, row)], LOWER[(mine, row)]

                def value(index):
                    return turned_ref[1, rows] if index == MIRROR else sums_ref[index, rows]

                @pl.when(jnp.logical_and(core == mine, z == target))
                def _():
                    for place, index in enumerate(upper):
                        upper_ref[place] = value(index)
                    for place in range(2):
                        lower_ref[place] = turned_ref[lower[min(place, len(lower) - 1)], rows]

                for step in range(1, 4):

                    @pl.when(jnp.logical_and(core == mine, (z + step) % 4 == target))
                    def _():
                        out_ref = out_refs[step - 1]
                        for place in range(BAND):
                            out_ref[place] = jnp.zeros((64, BW), BF16)
                        for place, index in enumerate(upper):
                            whole = value(index)
                            high = whole.astype(BF16)
                            out_ref[place] = high
                            if index == 0:
                                out_ref[BAND - 1] = (whole - high.astype(F32)).astype(BF16)
                        for place in range(2):
                            turned = turned_ref[lower[min(place, len(lower) - 1)], rows]
                            out_ref[BAND + place] = turned.astype(BF16)


def pack(own, arrived):
    upper = jax.ShapeDtypeStruct((BAND - 1, 64, BW), F32)
    lower = jax.ShapeDtypeStruct((2, 64, BW), F32)
    sent = jax.ShapeDtypeStruct((BAND + 2, 64, BW), BF16)
    return pl.pallas_call(
        pack_kernel,
        in_specs=[VMEM] * 4,
        out_specs=[VMEM] * 5,
        out_shape=[upper, lower] + [sent] * 3,
        scratch_shapes=[pltpu.VMEM((BAND, BW, BW), F32), pltpu.VMEM((BAND, BW, BW), F32)],
        compiler_params=SMALL,
    )(own, *arrived)


def split_kernel(upper_ref, lower_ref, *refs):
    arrived, turned_ref, kept_ref, sent_ref = refs[:3], refs[3], refs[4], refs[5]
    z, core, _ = place_here()
    for place in range(2):
        total = lower_ref[place]
        for source in arrived:
            total = total + source[BAND + place].astype(F32)
        turned_ref[place] = total
    for ref, part in ((kept_ref, core), (sent_ref, 1 - core)):
        rows = pl.ds(pl.multiple_of(part * 32, 32), 32)
        for place in range(BAND - 1):
            total = upper_ref[place, rows]
            for source in arrived:
                total = total + source[place, rows].astype(F32)
                if place == 0:
                    total = total + source[BAND - 1, rows].astype(F32)
            ref[place] = total


def split(upper, lower, arrived):
    half = jax.ShapeDtypeStruct((BAND - 1, 32, BW), F32)
    return pl.pallas_call(
        split_kernel,
        in_specs=[VMEM] * 5,
        out_specs=[VMEM] * 3,
        out_shape=[jax.ShapeDtypeStruct(lower.shape, F32), half, half],
        compiler_params=SMALL,
    )(upper, lower, *arrived)


def final_kernel(mask_ref, own_upper_ref, other_upper_ref, own_lower_ref, other_lower_ref, out_ref):
    z, core, _ = place_here()
    for row in range(2):
        for mine in range(2):

            @pl.when(jnp.logical_and(core == mine, z // 2 == row))
            def _():
                for half in range(2):
                    upper_ref = own_upper_ref if half == mine else other_upper_ref
                    lower_ref = own_lower_ref if half == mine else other_lower_ref
                    count = len(UPPER[(half, row)])
                    for place, slot in enumerate(SLOTS[(half, row)]):
                        if place < count:
                            value = upper_ref[place]
                        else:
                            value = lower_ref[place - count, mine * 32 : mine * 32 + 32]
                        columns = slice(slot * BW, (slot + 1) * BW)
                        out_ref[:, columns] = value * mask_ref[:, columns]


def final(mask, *pieces):
    return pl.pallas_call(
        final_kernel,
        in_specs=[VMEM] * 5,
        out_specs=VMEM,
        out_shape=jax.ShapeDtypeStruct(mask.shape, F32),
        compiler_params=SMALL,
    )(mask, *pieces)


def local(three_index, block_size, screen):
    flat = three_index.reshape(-1, three_index.shape[2])
    def exchanged(pieces):
        return jnp.concatenate([send(piece, core_pairs()) for piece in pieces])

    def passed(step, mine, other):
        outgoing = pair_sum(mine, other)
        return outgoing, send(outgoing, plane_pairs(step, True))

    mine, theirs, held = first_tiles(flat, STEPS[0])
    other = send(theirs, core_pairs())
    next_mine, *next_theirs = later_tiles(held, block_size, STEPS[1], 1)
    next_other = exchanged(next_theirs)
    sent1, arrived1 = passed(STEPS[0], mine, other)
    sent2, arrived2 = passed(STEPS[1], next_mine, next_other)
    mine, *theirs = later_tiles(held, sent2, STEPS[2], 2)
    other = exchanged(theirs)
    sent3, arrived3 = passed(STEPS[2], mine, other)
    mine, theirs, mask = last_tiles(block_size, screen, held, arrived1, STEPS[3])
    own, *outgoing = first_total(mine, send(theirs, core_pairs()), [arrived1, arrived2, arrived3])
    arrived = [send(outgoing[step - 1], plane_pairs(step, False)) for step in (2, 3, 1)]
    upper, lower, *outgoing = pack(own, arrived)
    arrived = [send(outgoing[step - 1], z_pairs(step)) for step in (2, 3, 1)]
    lower, upper, theirs = split(upper, lower, arrived)
    lower = send(lower, mirror_pairs())
    return final(mask, upper, send(theirs, core_pairs()), lower, send(lower, core_pairs()))


def solution(mesh):
    in_specs = (P(("aux", "bas"), None, None), P(), P())
    out_specs = P(("bas", "aux"), None)
    return jax.shard_map(local, mesh=mesh, in_specs=in_specs, out_specs=out_specs, check_vma=False)
```

```python
import functools
import math

import jax
import jax.numpy as jnp
from jax import lax
from jax.experimental import pallas as pl
from jax.experimental.pallas import tpu as pltpu
from jax.sharding import PartitionSpec as P

AUX = 6144
OCC = 32
BW = 128
BAND = 5
NB = 32
OWNERS = 16
PAIR = 2 * BW
AXES = ("aux", "bas")
F32 = jnp.float32
BF16 = jnp.bfloat16

TILES = (
    ((0, 0), (0, 2), (0, 3), (1, 1), (1, 2)),
    ((1, 0), (0, 1), (0, 4), (1, 3), (1, 4)),
)
MIRROR = BAND
UPPER = {(0, 0): (0, 1, 2), (1, 0): (1, 2), (0, 1): (3, 4), (1, 1): (0, 3, 4, MIRROR)}
LOWER = {(0, 0): (1, 3), (1, 0): (2, 3), (0, 1): (2, 4), (1, 1): (4,)}
SLOTS = {(0, 0): (4, 6, 7, 2, 3), (1, 0): (5, 8, 0, 1), (0, 1): (5, 6, 1, 2), (1, 1): (4, 7, 8, 3, 0)}
SLOT_COUNT = 2 * BAND - 1
LOWER_PLACES = (BAND, BAND - 2)
STEPS = (2, 1, 3, 0)


def device(z, c, y, x):
    return (z * 2 + c) * 16 + y * 4 + x


EVERY = [(z, c, y, x) for z in range(4) for c in range(2) for y in range(4) for x in range(4)]


def core_pairs():
    return [(device(z, c, y, x), device(z, 1 - c, y, x)) for z, c, y, x in EVERY]


def plane_pairs(step, first):
    pairs = []
    for z, c, y, x in EVERY:
        if (c == 0) == first:
            target = device(z, c, (y + step) % 4, x)
        else:
            target = device(z, c, y, (x + step) % 4)
        pairs.append((device(z, c, y, x), target))
    return pairs


def mirror_pairs():
    pairs = []
    for z, c, y, x in EVERY:
        owner = (y * 4 + x + 1 + c) % OWNERS
        pairs.append((device(z, c, y, x), device(z, c, owner // 4, owner % 4)))
    return pairs


def z_pairs(step):
    return [(device(z, c, y, x), device((z + step) % 4, c, y, x)) for z, c, y, x in EVERY]


def send(value, pairs):
    return lax.ppermute(value, AXES, pairs)


def place_here():
    aux = lax.axis_index("aux")
    bas = lax.axis_index("bas")
    return aux // 2, aux % 2, bas


def panel(ref, block, depth):
    return ref[depth, pl.ds(pl.multiple_of(block * PAIR, PAIR), PAIR)]


def gram(left, right):
    return lax.dot_general(left, right, (((0,), (0,)), ((), ())), preferred_element_type=F32)


def set_products(flat_ref, step, bas, depth):
    y, x = bas // 4, bas % 4
    for other in range(4):
        owner = ((y + step) % 4) * 4 + (x + other) % 4
        left = panel(flat_ref, owner, depth)
        right = panel(flat_ref, jnp.minimum(owner + 1, OWNERS - 1), depth)
        zero = gram(left[:, :BW], left[:, :BW]), gram(left, right)
        owner = ((y + other) % 4) * 4 + (x + step) % 4
        left = panel(flat_ref, owner, depth)
        right = panel(flat_ref, jnp.minimum(owner + 2, OWNERS - 1), depth)
        yield zero + (gram(left, left), gram(left, right))


def put_tiles(parts, position, core, mine_ref, theirs_ref):
    low, high = slice(0, BW), slice(BW, PAIR)
    diagonal, near, block, far = parts
    zero = diagonal, near[low, low], near[low, high], near[high, low], near[high, high]
    one = block[high, high], block[low, high], far[low, low], far[high, low], far[high, high]
    for place in range(BAND):
        first, second = zero[place].astype(BF16), one[place].astype(BF16)
        mine_ref[position, place] = jnp.where(core == 0, first, second)
        theirs_ref[0, place] = jnp.where(core == 0, second, first)


def depth_parts(depth):
    sizes = (depth // 3, depth // 3, depth // 6, depth // 6)
    return [pl.ds(sum(sizes[:index]), size) for index, size in enumerate(sizes)]


def first_kernel(flat_hbm, mine_ref, theirs_ref, flat_ref, small_ref, sums_ref, sems, *, step):
    z, core, bas = place_here()
    depths = depth_parts(flat_ref.shape[0])
    copies = [
        pltpu.make_async_copy(flat_hbm.at[depth], flat_ref.at[depth], sems.at[index])
        for index, depth in enumerate(depths)
    ]
    for copy in copies:
        copy.start()
    for index, (copy, depth) in enumerate(zip(copies, depths)):
        copy.wait()
        for position, parts in enumerate(set_products(flat_ref, step, bas, depth)):
            if index > 0:
                before = (small_ref[position], *(sums_ref[position, place] for place in range(3)))
                parts = [total + part for total, part in zip(before, parts)]
            if index < len(depths) - 1:
                small_ref[position] = parts[0]
                for place, part in enumerate(parts[1:]):
                    sums_ref[position, place] = part
            else:
                put_tiles(parts, position, core, mine_ref, theirs_ref.at[pl.ds(position, 1)])


def later_kernel(flat_ref, after_ref, mine_ref, *theirs_refs, step):
    z, core, bas = place_here()
    for position, parts in enumerate(set_products(flat_ref, step, bas, pl.ds(0, flat_ref.shape[0]))):
        size = 4 // len(theirs_refs)
        theirs_ref = theirs_refs[position // size].at[pl.ds(position % size, 1)]
        put_tiles(parts, position, core, mine_ref, theirs_ref)


def last_kernel(size_ref, screen_ref, flat_ref, after_ref, mine_ref, theirs_ref, mask_ref, *, step, factor):
    later_kernel(flat_ref, after_ref, mine_ref, theirs_ref, step=step)
    z, core, bas = place_here()
    block = bas * 2 + z // 2
    rows = lax.broadcasted_iota(jnp.int32, (32, BW), 0) + (z % 2) * 64 + core * 32
    columns = lax.broadcasted_iota(jnp.int32, (32, BW), 1)
    row_mask = rows < size_ref[block]
    for slot in range(SLOT_COUNT):
        offset = slot - (BAND - 1)
        partner = jnp.clip(block + offset, 0, NB - 1)
        inside = jnp.logical_and(block + offset >= 0, block + offset < NB)
        kept = jnp.where(inside, screen_ref[abs(offset), jnp.minimum(block, partner)], 0)
        limit = jnp.where(kept > 0, size_ref[partner], 0)
        mask = jnp.logical_and(row_mask, columns < limit)
        mask_ref[:, slot * BW : (slot + 1) * BW] = jnp.where(mask, factor, 0.0)


VMEM = pl.BlockSpec(memory_space=pltpu.VMEM)
ANYWHERE = pl.BlockSpec(memory_space=pl.ANY)
SMALL = pltpu.CompilerParams(vmem_limit_bytes=4 << 20)
SCALARS = pl.BlockSpec(memory_space=pltpu.SMEM)


SET = jax.ShapeDtypeStruct((4, BAND, BW, BW), BF16)


def cost(depth, moved=0):
    return pl.CostEstimate(
        flops=4 * 13 * PAIR * PAIR * depth // 2, bytes_accessed=moved, transcendentals=0
    )


def first_tiles(flat, step):
    depth = flat.shape[0]
    return pl.pallas_call(
        functools.partial(first_kernel, step=step),
        in_specs=[ANYWHERE],
        out_specs=[VMEM, VMEM, VMEM],
        out_shape=[SET, SET, pltpu.VMEM(flat.shape, BF16)],
        scratch_shapes=[
            pltpu.VMEM((4, BW, BW), F32),
            pltpu.VMEM((4, 3, PAIR, PAIR), F32),
            pltpu.SemaphoreType.DMA((4,)),
        ],
        compiler_params=pltpu.CompilerParams(vmem_limit_bytes=20 << 20),
        cost_estimate=cost(depth, flat.size * 2),
    )(pltpu.with_memory_space_constraint(flat, pltpu.HBM))


def later_tiles(flat, after, step, pieces=1):
    return pl.pallas_call(
        functools.partial(later_kernel, step=step),
        in_specs=[VMEM, ANYWHERE],
        out_specs=[VMEM] * (1 + pieces),
        out_shape=[SET] + [jax.ShapeDtypeStruct((4 // pieces, BAND, BW, BW), BF16)] * pieces,
        compiler_params=pltpu.CompilerParams(vmem_limit_bytes=16 << 20),
        cost_estimate=cost(flat.shape[0]),
    )(flat, after)


def last_tiles(block_size, screen, flat, after, step):
    factor = 1.0 / math.sqrt(AUX * OCC)
    return pl.pallas_call(
        functools.partial(last_kernel, step=step, factor=factor),
        in_specs=[SCALARS, SCALARS, VMEM, ANYWHERE],
        out_specs=[VMEM] * 3,
        out_shape=[SET, SET, jax.ShapeDtypeStruct((32, SLOT_COUNT * BW), F32)],
        compiler_params=pltpu.CompilerParams(vmem_limit_bytes=16 << 20),
        cost_estimate=cost(flat.shape[0]),
    )(block_size, screen.T, flat, after)


def total_kernel(*refs):
    mine_ref, other_ref, *arrived, own_ref, first_ref, second_ref, third_ref = refs
    for position, out_ref in enumerate((own_ref, first_ref, second_ref, third_ref)):
        total = mine_ref[position].astype(F32) + other_ref[position].astype(F32)
        for ref in arrived:
            total = total + ref[position].astype(F32)
        out_ref[...] = total.astype(out_ref.dtype)


def first_total(mine, other, arrived):
    sent = jax.ShapeDtypeStruct((BAND, BW, BW), BF16)
    return pl.pallas_call(
        total_kernel,
        in_specs=[VMEM] * 5,
        out_specs=[VMEM] * 4,
        out_shape=[jax.ShapeDtypeStruct((BAND, BW, BW), F32), sent, sent, sent],
        compiler_params=SMALL,
    )(mine, other, *arrived)


def pair_sum(mine, other):
    return (mine.astype(F32) + other.astype(F32)).astype(BF16)


def pack_kernel(own_ref, first_ref, second_ref, third_ref, upper_ref, lower_ref, *refs):
    out_refs, sums_ref, turned_ref = refs[:3], refs[3], refs[4]
    z, core, _ = place_here()
    for index in range(BAND):
        total = own_ref[index]
        for ref in (first_ref, second_ref, third_ref):
            total = total + ref[index].astype(F32)
        sums_ref[index] = total
        if index > 0:
            turned_ref[index] = total.T
    for mine in range(2):
        for row in range(2):
            for half in range(2):
                target = row * 2 + half
                rows = pl.ds(half * 64, 64)
                upper, lower = UPPER[(mine, row)], LOWER[(mine, row)]

                def value(index):
                    return turned_ref[1, rows] if index == MIRROR else sums_ref[index, rows]

                @pl.when(jnp.logical_and(core == mine, z == target))
                def _():
                    for place in range(BAND - 1):
                        upper_ref[place] = value(upper[place]) if place < len(upper) else jnp.zeros((64, BW), F32)
                    for place in range(2):
                        lower_ref[place] = turned_ref[lower[min(place, len(lower) - 1)], rows]

                for step in range(1, 4):

                    @pl.when(jnp.logical_and(core == mine, (z + step) % 4 == target))
                    def _():
                        out_ref = out_refs[step - 1]
                        for place in range(BAND + 1):
                            out_ref[place] = jnp.zeros((64, BW), BF16)
                        for place, index in enumerate(upper):
                            whole = value(index)
                            high = whole.astype(BF16)
                            out_ref[place] = high
                            if index == 0:
                                out_ref[BAND - 1] = (whole - high.astype(F32)).astype(BF16)
                        for place, index in zip(LOWER_PLACES, lower):
                            out_ref[place] = turned_ref[index, rows].astype(BF16)


def pack(own, arrived):
    upper = jax.ShapeDtypeStruct((BAND - 1, 64, BW), F32)
    lower = jax.ShapeDtypeStruct((2, 64, BW), F32)
    sent = jax.ShapeDtypeStruct((BAND + 1, 64, BW), BF16)
    return pl.pallas_call(
        pack_kernel,
        in_specs=[VMEM] * 4,
        out_specs=[VMEM] * 5,
        out_shape=[upper, lower] + [sent] * 3,
        scratch_shapes=[pltpu.VMEM((BAND, BW, BW), F32), pltpu.VMEM((BAND, BW, BW), F32)],
        compiler_params=SMALL,
    )(own, *arrived)


def split_kernel(upper_ref, lower_ref, *refs):
    arrived, turned_ref, kept_ref, sent_ref = refs[:3], refs[3], refs[4], refs[5]
    z, core, _ = place_here()
    for place in range(2):
        total = lower_ref[place]
        for source in arrived:
            total = total + source[LOWER_PLACES[place]].astype(F32)
        turned_ref[place] = total
    for ref, part in ((kept_ref, core), (sent_ref, 1 - core)):
        rows = pl.ds(pl.multiple_of(part * 32, 32), 32)
        for place in range(BAND - 1):
            total = upper_ref[place, rows]
            for source in arrived:
                total = total + source[place, rows].astype(F32)
                if place == 0:
                    total = total + source[BAND - 1, rows].astype(F32)
            ref[place] = total


def split(upper, lower, arrived):
    half = jax.ShapeDtypeStruct((BAND - 1, 32, BW), F32)
    return pl.pallas_call(
        split_kernel,
        in_specs=[VMEM] * 5,
        out_specs=[VMEM] * 3,
        out_shape=[jax.ShapeDtypeStruct(lower.shape, F32), half, half],
        compiler_params=SMALL,
    )(upper, lower, *arrived)


def final_kernel(mask_ref, own_upper_ref, other_upper_ref, own_lower_ref, other_lower_ref, out_ref):
    z, core, _ = place_here()
    for row in range(2):
        for mine in range(2):

            @pl.when(jnp.logical_and(core == mine, z // 2 == row))
            def _():
                for half in range(2):
                    upper_ref = own_upper_ref if half == mine else other_upper_ref
                    lower_ref = own_lower_ref if half == mine else other_lower_ref
                    count = len(UPPER[(half, row)])
                    for place, slot in enumerate(SLOTS[(half, row)]):
                        if place < count:
                            value = upper_ref[place]
                        else:
                            value = lower_ref[place - count, mine * 32 : mine * 32 + 32]
                        columns = slice(slot * BW, (slot + 1) * BW)
                        out_ref[:, columns] = value * mask_ref[:, columns]


def final(mask, *pieces):
    return pl.pallas_call(
        final_kernel,
        in_specs=[VMEM] * 5,
        out_specs=VMEM,
        out_shape=jax.ShapeDtypeStruct(mask.shape, F32),
        compiler_params=SMALL,
    )(mask, *pieces)


def local(three_index, block_size, screen):
    flat = three_index.reshape(-1, three_index.shape[2])
    def exchanged(pieces):
        return jnp.concatenate([send(piece, core_pairs()) for piece in pieces])

    def passed(step, mine, other):
        outgoing = pair_sum(mine, other)
        return outgoing, send(outgoing, plane_pairs(step, True))

    mine, theirs, held = first_tiles(flat, STEPS[0])
    other = send(theirs, core_pairs())
    next_mine, *next_theirs = later_tiles(held, block_size, STEPS[1], 1)
    next_other = exchanged(next_theirs)
    sent1, arrived1 = passed(STEPS[0], mine, other)
    sent2, arrived2 = passed(STEPS[1], next_mine, next_other)
    mine, *theirs = later_tiles(held, sent2, STEPS[2], 2)
    other = exchanged(theirs)
    sent3, arrived3 = passed(STEPS[2], mine, other)
    mine, theirs, mask = last_tiles(block_size, screen, held, arrived1, STEPS[3])
    own, *outgoing = first_total(mine, send(theirs, core_pairs()), [arrived1, arrived2, arrived3])
    arrived = [send(outgoing[step - 1], plane_pairs(step, False)) for step in (2, 3, 1)]
    upper, lower, *outgoing = pack(own, arrived)
    arrived = [send(outgoing[step - 1], z_pairs(step)) for step in (1, 3, 2)]
    lower, upper, theirs = split(upper, lower, arrived)
    lower = send(lower, mirror_pairs())
    return final(mask, upper, send(theirs, core_pairs()), lower, send(lower, core_pairs()))


def solution(mesh):
    in_specs = (P(("aux", "bas"), None, None), P(), P())
    out_specs = P(("bas", "aux"), None)
    return jax.shard_map(local, mesh=mesh, in_specs=in_specs, out_specs=out_specs, check_vma=False)
```

```python
import functools
import math

import jax
import jax.numpy as jnp
from jax import lax
from jax.experimental import pallas as pl
from jax.experimental.pallas import tpu as pltpu
from jax.sharding import PartitionSpec as P

AUX = 6144
OCC = 32
BW = 128
BAND = 5
NB = 32
OWNERS = 16
PAIR = 2 * BW
AXES = ("aux", "bas")
F32 = jnp.float32
BF16 = jnp.bfloat16

TILES = (
    ((0, 0), (0, 2), (0, 3), (1, 1), (1, 2)),
    ((1, 0), (0, 1), (0, 4), (1, 3), (1, 4)),
)
MIRROR = BAND
UPPER = {(0, 0): (0, 1, 2), (1, 0): (1, 2), (0, 1): (3, 4), (1, 1): (0, 3, 4, MIRROR)}
LOWER = {(0, 0): (1, 3), (1, 0): (2, 3), (0, 1): (2, 4), (1, 1): (4,)}
SLOTS = {(0, 0): (4, 6, 7, 2, 3), (1, 0): (5, 8, 0, 1), (0, 1): (5, 6, 1, 2), (1, 1): (4, 7, 8, 3, 0)}
SLOT_COUNT = 2 * BAND - 1
LOWER_PLACES = (BAND, BAND - 2)
STEPS = (2, 1, 3, 0)


def device(z, c, y, x):
    return (z * 2 + c) * 16 + y * 4 + x


EVERY = [(z, c, y, x) for z in range(4) for c in range(2) for y in range(4) for x in range(4)]


def core_pairs():
    return [(device(z, c, y, x), device(z, 1 - c, y, x)) for z, c, y, x in EVERY]


def plane_pairs(step, first):
    pairs = []
    for z, c, y, x in EVERY:
        if (c == 0) == first:
            target = device(z, c, (y + step) % 4, x)
        else:
            target = device(z, c, y, (x + step) % 4)
        pairs.append((device(z, c, y, x), target))
    return pairs


def mirror_pairs():
    pairs = []
    for z, c, y, x in EVERY:
        owner = (y * 4 + x + 1 + c) % OWNERS
        pairs.append((device(z, c, y, x), device(z, c, owner // 4, owner % 4)))
    return pairs


def z_pairs(step):
    return [(device(z, c, y, x), device((z + step) % 4, c, y, x)) for z, c, y, x in EVERY]


def send(value, pairs):
    return lax.ppermute(value, AXES, pairs)


def place_here():
    aux = lax.axis_index("aux")
    bas = lax.axis_index("bas")
    return aux // 2, aux % 2, bas


def panel(ref, block, depth):
    return ref[depth, pl.ds(pl.multiple_of(block * PAIR, PAIR), PAIR)]


def gram(left, right):
    return lax.dot_general(left, right, (((0,), (0,)), ((), ())), preferred_element_type=F32)


def set_products(flat_ref, step, bas, depth):
    y, x = bas // 4, bas % 4
    for other in range(4):
        owner = ((y + step) % 4) * 4 + (x + other) % 4
        left = panel(flat_ref, owner, depth)
        right = panel(flat_ref, jnp.minimum(owner + 1, OWNERS - 1), depth)
        zero = gram(left[:, :BW], left[:, :BW]), gram(left, right)
        owner = ((y + other) % 4) * 4 + (x + step) % 4
        left = panel(flat_ref, owner, depth)
        right = panel(flat_ref, jnp.minimum(owner + 2, OWNERS - 1), depth)
        yield zero + (gram(left, left), gram(left, right))


def put_tiles(parts, position, core, mine_ref, theirs_ref):
    low, high = slice(0, BW), slice(BW, PAIR)
    diagonal, near, block, far = parts
    zero = diagonal, near[low, low], near[low, high], near[high, low], near[high, high]
    one = block[high, high], block[low, high], far[low, low], far[high, low], far[high, high]
    for place in range(BAND):
        first, second = zero[place].astype(BF16), one[place].astype(BF16)
        mine_ref[position, place] = jnp.where(core == 0, first, second)
        theirs_ref[0, place] = jnp.where(core == 0, second, first)


def depth_parts(depth):
    sizes = (depth // 2, depth // 3, depth // 6)
    return [pl.ds(sum(sizes[:index]), size) for index, size in enumerate(sizes)]


def first_kernel(flat_hbm, mine_ref, theirs_ref, flat_ref, small_ref, sums_ref, sems, *, step):
    z, core, bas = place_here()
    depths = depth_parts(flat_ref.shape[0])
    copies = [
        pltpu.make_async_copy(flat_hbm.at[depth], flat_ref.at[depth], sems.at[index])
        for index, depth in enumerate(depths)
    ]
    for copy in copies:
        copy.start()
    for index, (copy, depth) in enumerate(zip(copies, depths)):
        copy.wait()
        for position, parts in enumerate(set_products(flat_ref, step, bas, depth)):
            if index > 0:
                before = (small_ref[position], *(sums_ref[position, place] for place in range(3)))
                parts = [total + part for total, part in zip(before, parts)]
            if index < len(depths) - 1:
                small_ref[position] = parts[0]
                for place, part in enumerate(parts[1:]):
                    sums_ref[position, place] = part
            else:
                put_tiles(parts, position, core, mine_ref, theirs_ref.at[pl.ds(position, 1)])


def later_kernel(flat_ref, after_ref, mine_ref, *theirs_refs, step):
    z, core, bas = place_here()
    for position, parts in enumerate(set_products(flat_ref, step, bas, pl.ds(0, flat_ref.shape[0]))):
        size = 4 // len(theirs_refs)
        theirs_ref = theirs_refs[position // size].at[pl.ds(position % size, 1)]
        put_tiles(parts, position, core, mine_ref, theirs_ref)


def last_kernel(size_ref, screen_ref, flat_ref, after_ref, mine_ref, theirs_ref, mask_ref, *, step, factor):
    later_kernel(flat_ref, after_ref, mine_ref, theirs_ref, step=step)
    z, core, bas = place_here()
    block = bas * 2 + z // 2
    rows = lax.broadcasted_iota(jnp.int32, (32, BW), 0) + (z % 2) * 64 + core * 32
    columns = lax.broadcasted_iota(jnp.int32, (32, BW), 1)
    row_mask = rows < size_ref[block]
    for slot in range(SLOT_COUNT):
        offset = slot - (BAND - 1)
        partner = jnp.clip(block + offset, 0, NB - 1)
        inside = jnp.logical_and(block + offset >= 0, block + offset < NB)
        kept = jnp.where(inside, screen_ref[abs(offset), jnp.minimum(block, partner)], 0)
        limit = jnp.where(kept > 0, size_ref[partner], 0)
        mask = jnp.logical_and(row_mask, columns < limit)
        mask_ref[:, slot * BW : (slot + 1) * BW] = jnp.where(mask, factor, 0.0)


VMEM = pl.BlockSpec(memory_space=pltpu.VMEM)
ANYWHERE = pl.BlockSpec(memory_space=pl.ANY)
SMALL = pltpu.CompilerParams(vmem_limit_bytes=4 << 20)
SCALARS = pl.BlockSpec(memory_space=pltpu.SMEM)


SET = jax.ShapeDtypeStruct((4, BAND, BW, BW), BF16)


def cost(depth, moved=0):
    return pl.CostEstimate(
        flops=4 * 13 * PAIR * PAIR * depth // 2, bytes_accessed=moved, transcendentals=0
    )


def first_tiles(flat, step):
    depth = flat.shape[0]
    return pl.pallas_call(
        functools.partial(first_kernel, step=step),
        in_specs=[ANYWHERE],
        out_specs=[VMEM, VMEM, VMEM],
        out_shape=[SET, SET, pltpu.VMEM(flat.shape, BF16)],
        scratch_shapes=[
            pltpu.VMEM((4, BW, BW), F32),
            pltpu.VMEM((4, 3, PAIR, PAIR), F32),
            pltpu.SemaphoreType.DMA((3,)),
        ],
        compiler_params=pltpu.CompilerParams(vmem_limit_bytes=20 << 20),
        cost_estimate=cost(depth, flat.size * 2),
    )(pltpu.with_memory_space_constraint(flat, pltpu.HBM))


def later_tiles(flat, after, step, pieces=1):
    return pl.pallas_call(
        functools.partial(later_kernel, step=step),
        in_specs=[VMEM, ANYWHERE],
        out_specs=[VMEM] * (1 + pieces),
        out_shape=[SET] + [jax.ShapeDtypeStruct((4 // pieces, BAND, BW, BW), BF16)] * pieces,
        compiler_params=pltpu.CompilerParams(vmem_limit_bytes=16 << 20),
        cost_estimate=cost(flat.shape[0]),
    )(flat, after)


def last_tiles(block_size, screen, flat, after, step):
    factor = 1.0 / math.sqrt(AUX * OCC)
    return pl.pallas_call(
        functools.partial(last_kernel, step=step, factor=factor),
        in_specs=[SCALARS, SCALARS, VMEM, ANYWHERE],
        out_specs=[VMEM] * 3,
        out_shape=[SET, SET, jax.ShapeDtypeStruct((32, SLOT_COUNT * BW), F32)],
        compiler_params=pltpu.CompilerParams(vmem_limit_bytes=16 << 20),
        cost_estimate=cost(flat.shape[0]),
    )(block_size, screen.T, flat, after)


def total_kernel(*refs):
    mine_ref, other_ref, *arrived, own_ref, first_ref, second_ref, third_ref = refs
    for position, out_ref in enumerate((own_ref, first_ref, second_ref, third_ref)):
        total = mine_ref[position].astype(F32) + other_ref[position].astype(F32)
        for ref in arrived:
            total = total + ref[position].astype(F32)
        out_ref[...] = total.astype(out_ref.dtype)


def first_total(mine, other, arrived):
    sent = jax.ShapeDtypeStruct((BAND, BW, BW), BF16)
    return pl.pallas_call(
        total_kernel,
        in_specs=[VMEM] * 5,
        out_specs=[VMEM] * 4,
        out_shape=[jax.ShapeDtypeStruct((BAND, BW, BW), F32), sent, sent, sent],
        compiler_params=SMALL,
    )(mine, other, *arrived)


def pair_sum(mine, other):
    return (mine.astype(F32) + other.astype(F32)).astype(BF16)


def pack_kernel(own_ref, first_ref, second_ref, third_ref, upper_ref, lower_ref, *refs):
    out_refs, sums_ref, turned_ref = refs[:3], refs[3], refs[4]
    z, core, _ = place_here()
    for index in range(BAND):
        total = own_ref[index]
        for ref in (first_ref, second_ref, third_ref):
            total = total + ref[index].astype(F32)
        sums_ref[index] = total
        if index > 0:
            turned_ref[index] = total.T
    for mine in range(2):
        for row in range(2):
            for half in range(2):
                target = row * 2 + half
                rows = pl.ds(half * 64, 64)
                upper, lower = UPPER[(mine, row)], LOWER[(mine, row)]

                def value(index):
                    return turned_ref[1, rows] if index == MIRROR else sums_ref[index, rows]

                @pl.when(jnp.logical_and(core == mine, z == target))
                def _():
                    for place in range(BAND - 1):
                        upper_ref[place] = value(upper[place]) if place < len(upper) else jnp.zeros((64, BW), F32)
                    for place in range(2):
                        lower_ref[place] = turned_ref[lower[min(place, len(lower) - 1)], rows]

                for step in range(1, 4):

                    @pl.when(jnp.logical_and(core == mine, (z + step) % 4 == target))
                    def _():
                        out_ref = out_refs[step - 1]
                        for place in range(BAND + 1):
                            out_ref[place] = jnp.zeros((64, BW), BF16)
                        for place, index in enumerate(upper):
                            whole = value(index)
                            high = whole.astype(BF16)
                            out_ref[place] = high
                            if index == 0:
                                out_ref[BAND - 1] = (whole - high.astype(F32)).astype(BF16)
                        for place, index in zip(LOWER_PLACES, lower):
                            out_ref[place] = turned_ref[index, rows].astype(BF16)


def pack(own, arrived):
    upper = jax.ShapeDtypeStruct((BAND - 1, 64, BW), F32)
    lower = jax.ShapeDtypeStruct((2, 64, BW), F32)
    sent = jax.ShapeDtypeStruct((BAND + 1, 64, BW), BF16)
    return pl.pallas_call(
        pack_kernel,
        in_specs=[VMEM] * 4,
        out_specs=[VMEM] * 5,
        out_shape=[upper, lower] + [sent] * 3,
        scratch_shapes=[pltpu.VMEM((BAND, BW, BW), F32), pltpu.VMEM((BAND, BW, BW), F32)],
        compiler_params=SMALL,
    )(own, *arrived)


def split_kernel(upper_ref, lower_ref, *refs):
    arrived, turned_ref, kept_ref, sent_ref = refs[:3], refs[3], refs[4], refs[5]
    z, core, _ = place_here()
    for place in range(2):
        total = lower_ref[place]
        for source in arrived:
            total = total + source[LOWER_PLACES[place]].astype(F32)
        turned_ref[place] = total
    for ref, part in ((kept_ref, core), (sent_ref, 1 - core)):
        rows = pl.ds(pl.multiple_of(part * 32, 32), 32)
        for place in range(BAND - 1):
            total = upper_ref[place, rows]
            for source in arrived:
                total = total + source[place, rows].astype(F32)
                if place == 0:
                    total = total + source[BAND - 1, rows].astype(F32)
            ref[place] = total


def split(upper, lower, arrived):
    half = jax.ShapeDtypeStruct((BAND - 1, 32, BW), F32)
    return pl.pallas_call(
        split_kernel,
        in_specs=[VMEM] * 5,
        out_specs=[VMEM] * 3,
        out_shape=[jax.ShapeDtypeStruct(lower.shape, F32), half, half],
        compiler_params=SMALL,
    )(upper, lower, *arrived)


def final_kernel(mask_ref, own_upper_ref, other_upper_ref, own_lower_ref, other_lower_ref, out_ref):
    z, core, _ = place_here()
    for row in range(2):
        for mine in range(2):

            @pl.when(jnp.logical_and(core == mine, z // 2 == row))
            def _():
                for half in range(2):
                    upper_ref = own_upper_ref if half == mine else other_upper_ref
                    lower_ref = own_lower_ref if half == mine else other_lower_ref
                    count = len(UPPER[(half, row)])
                    for place, slot in enumerate(SLOTS[(half, row)]):
                        if place < count:
                            value = upper_ref[place]
                        else:
                            value = lower_ref[place - count, mine * 32 : mine * 32 + 32]
                        columns = slice(slot * BW, (slot + 1) * BW)
                        out_ref[:, columns] = value * mask_ref[:, columns]


def final(mask, *pieces):
    return pl.pallas_call(
        final_kernel,
        in_specs=[VMEM] * 5,
        out_specs=VMEM,
        out_shape=jax.ShapeDtypeStruct(mask.shape, F32),
        compiler_params=SMALL,
    )(mask, *pieces)


def local(three_index, block_size, screen):
    flat = three_index.reshape(-1, three_index.shape[2])
    def exchanged(pieces):
        return jnp.concatenate([send(piece, core_pairs()) for piece in pieces])

    def passed(step, mine, other):
        outgoing = pair_sum(mine, other)
        return outgoing, send(outgoing, plane_pairs(step, True))

    mine, theirs, held = first_tiles(flat, STEPS[0])
    other = send(theirs, core_pairs())
    next_mine, *next_theirs = later_tiles(held, block_size, STEPS[1], 1)
    next_other = exchanged(next_theirs)
    sent1, arrived1 = passed(STEPS[0], mine, other)
    sent2, arrived2 = passed(STEPS[1], next_mine, next_other)
    mine, *theirs = later_tiles(held, sent2, STEPS[2], 2)
    other = exchanged(theirs)
    sent3, arrived3 = passed(STEPS[2], mine, other)
    mine, theirs, mask = last_tiles(block_size, screen, held, arrived1, STEPS[3])
    own, *outgoing = first_total(mine, send(theirs, core_pairs()), [arrived1, arrived2, arrived3])
    arrived = [send(outgoing[step - 1], plane_pairs(step, False)) for step in (2, 3, 1)]
    upper, lower, *outgoing = pack(own, arrived)
    arrived = [send(outgoing[step - 1], z_pairs(step)) for step in (1, 3, 2)]
    lower, upper, theirs = split(upper, lower, arrived)
    lower = send(lower, mirror_pairs())
    return final(mask, upper, send(theirs, core_pairs()), lower, send(lower, core_pairs()))


def solution(mesh):
    in_specs = (P(("aux", "bas"), None, None), P(), P())
    out_specs = P(("bas", "aux"), None)
    return jax.shard_map(local, mesh=mesh, in_specs=in_specs, out_specs=out_specs, check_vma=False)
```
